128 devices in a mesh: seq: 32 (over y, x, core), head: 4 (over z).
Axes of the slice: x: 4, y: 4, z: 4, core: 2. Of those that a mesh axis runs over, the one named last changes fastest.
Arguments:
- query_matrix_rows: bfloat16 [8192, 2048], P('seq', 'head'), may hold values from -6 to 6
- key_matrix_rows: bfloat16 [8192, 2048], P('seq', 'head'), may hold values from -6 to 6
- value_matrix_rows: bfloat16 [8192, 4096], P('seq', 'head'), may hold values from -6 to 6
- write_strength: float32 [32, 8192], P('head', 'seq'), may hold values from 0 to 1
- forget_gate_code: int32 [32, 8192], P('head', 'seq'), may hold values from 0 to 52
- value_to_key_head: int32 [32], P('head'), may hold values from 0 to 15, as said below
- output_norm_gain: float32 [128], replicated, may hold values from 0.1 to 1.9
- output_weight: bfloat16 [4096, 2048], P('head'), may hold values from -0.09375 to 0.09375
- adapter_lowering: float32 [16, 4096], P(None, 'head'), may hold values from -0.09375 to 0.09375
- adapter_raising: float32 [16, 2048], replicated, may hold values from -1.5 to 1.5
- output_gradient: bfloat16 [8192, 2048], P('seq'), may hold values from -6 to 6
Outputs:
- grad_query: float32 [8192, 2048], P('seq', 'head')
- grad_key: float32 [8192, 2048], P('seq', 'head')
- grad_value: float32 [8192, 4096], P('seq', 'head')
- grad_rate: float32 [32, 8192], P('head', 'seq')
- grad_down: float32 [16, 4096], P(None, 'head')
- raising_gradient: float32 [16, 2048], replicated
The draws below stay inside these ranges and needn't reach their ends.
Inputs may be any that keep to these rules, and one draw needn't show every extreme that they name: `value_to_key_head`: value heads g * 8 to g * 8 + 7 read only key heads g * 4 to g * 4 + 3, each of these exactly 8 // 4 times.
All inputs are finite; a program needn't handle non-finite values.
Results may differ from the reference program's by a relative error of at most 0.00035.
Values sent between devices are 32-bit elements; how exact they have to be, the bound alone decides.
A program may use at most 192 MiB of HBM per device.

```python
import math
import jax
import jax.numpy as jnp
from jax import lax

MODEL_WIDTH = 2048
VALUE_HEADS = 32
HK = 16
DK = 128
VALUE_HEAD_SIZE = 128
ADAPTER_RANK = 16
BLOCK = 64
TOK_DEV = 256
TOKENS = 8192
HV_DEV = 8
HK_DEV = 4
N_HEAD = 4


def draw_write_strength(key, part):
    key = jax.random.fold_in(key, 11)
    base_key, device_key, rough_key = jax.random.split(key, 3)
    low_rate, high_rate = (0.0005, 0.3)
    base = jnp.exp(jax.random.uniform(base_key, (VALUE_HEADS, 1), jnp.float32, math.log(low_rate), math.log(high_rate)))
    device_level = jnp.exp(jax.random.uniform(device_key, (VALUE_HEADS, TOKENS // TOK_DEV), jnp.float32, math.log(0.5), math.log(2.0)))
    device_level = jnp.repeat(device_level, TOK_DEV, axis=1)
    rough = jax.random.uniform(rough_key, (VALUE_HEADS, TOKENS), jnp.float32, 0.5, 1.5)
    return (base * device_level * rough).astype(jnp.float32)


def draw_forget_gate_code(key, part):
    key = jax.random.fold_in(key, 17)
    level_key, jitter_key = jax.random.split(key, 2)
    levels = jax.random.randint(level_key, (VALUE_HEADS, TOKENS // TOK_DEV), 0, 53)
    levels = jnp.repeat(levels, TOK_DEV, axis=1)
    jitter = jax.random.randint(jitter_key, (VALUE_HEADS, TOKENS), -6, 7)
    return jnp.clip(levels + jitter, 0, 52).astype(jnp.int32)


def draw_value_to_key_head(key, part):
    key = jax.random.fold_in(key, 5)
    group_keys = jax.random.split(key, N_HEAD)

    def group_order(group_key):
        return jax.random.permutation(group_key, HV_DEV)
    orders = jax.vmap(group_order)(group_keys)
    ratio = HV_DEV // HK_DEV
    offsets = jnp.arange(N_HEAD, dtype=jnp.int32)[:, None] * HK_DEV
    return (orders // ratio + offsets).reshape(VALUE_HEADS).astype(jnp.int32)


def level_of(rng, shape, cuts, low, high):
    def one(axis_at, parts):
        draws = jax.random.uniform(jax.random.fold_in(jax.random.fold_in(rng, 6), axis_at), (parts,), jnp.float32, low / len(cuts), high / len(cuts))
        return jnp.repeat(jnp.exp(draws), shape[axis_at] // parts).reshape((-1,) + (1,) * (len(shape) - axis_at - 1))

    gain = one(*cuts[0])
    for cut in cuts[1:]:
        gain = gain * one(*cut)
    return gain


def bell_draw(own_key, extent, scale, most, cuts=(), held_as=jnp.bfloat16):
    values = scale * jax.random.normal(own_key, extent, jnp.float32)
    if cuts:
        values = values * level_of(own_key, extent, cuts, -0.22, 0.18)
    return jnp.clip(values, -most, most).astype(held_as)


def setup_inputs(seed: int = 0) -> dict:
    key_of = jax.random.split(jax.random.key(seed), 12)
    return {
        "query_matrix_rows": bell_draw(key_of[0], (TOKENS, HK * DK), 1.0, 6.0, ((0, 32), (1, 4))),
        "key_matrix_rows": bell_draw(key_of[1], (TOKENS, HK * DK), 1.0, 6.0, ((0, 32), (1, 4))),
        "value_matrix_rows": bell_draw(key_of[2], (TOKENS, VALUE_HEADS * VALUE_HEAD_SIZE), 1.0, 6.0, ((0, 32), (1, 4))),
        "write_strength": draw_write_strength(jax.random.fold_in(key_of[11], 71), 0),
        "forget_gate_code": draw_forget_gate_code(jax.random.fold_in(key_of[11], 71), 0),
        "value_to_key_head": draw_value_to_key_head(jax.random.fold_in(key_of[11], 71), 0),
        "output_norm_gain": jnp.clip(1.0 + 0.18 * jax.random.normal(key_of[6], (VALUE_HEAD_SIZE,), jnp.float32), 0.1, 1.9),
        "output_weight": bell_draw(key_of[7], (VALUE_HEADS * VALUE_HEAD_SIZE, MODEL_WIDTH), (VALUE_HEADS * VALUE_HEAD_SIZE) ** -0.5, 0.09375, ((0, 4),)),
        "adapter_lowering": bell_draw(key_of[8], (ADAPTER_RANK, VALUE_HEADS * VALUE_HEAD_SIZE), (VALUE_HEADS * VALUE_HEAD_SIZE) ** -0.5, 0.09375, ((1, 4),), jnp.float32),
        "adapter_raising": bell_draw(key_of[9], (ADAPTER_RANK, MODEL_WIDTH), ADAPTER_RANK ** -0.5, 1.5, (), jnp.float32),
        "output_gradient": bell_draw(key_of[10], (TOKENS, MODEL_WIDTH), 1.0, 6.0, ((0, 32),)),
    }


adapter_scale = 2.0

def unit_rows(array):
    return array * lax.rsqrt(lax.optimization_barrier(jnp.sum(array * array, axis=-1, keepdims=True)) + 1e-06)

def block_step(state, block_items):
    query_block, key_block, value_block, rate_block, log_block = block_items
    finest_precision = lax.Precision.HIGHEST
    cumlog = jnp.cumsum(log_block, axis=-1)
    width = log_block.shape[-1]
    row_index = jnp.arange(width)[:, None]
    col_index = jnp.arange(width)[None, :]
    gap_log = cumlog[..., :, None] - cumlog[..., None, :]
    decays = jnp.exp(jnp.where(row_index >= col_index, gap_log, 0.0))
    key_dots = jnp.einsum('hcd,hed->hce', key_block, key_block, precision=finest_precision)
    strict_part = jnp.where(row_index > col_index, decays * key_dots * rate_block[..., None, :], 0.0)
    identity = jnp.eye(width, dtype=strict_part.dtype)
    start_decay = jnp.exp(cumlog)[..., None]
    targets = value_block - start_decay * jnp.einsum('hcd,hdw->hcw', key_block, state, precision=finest_precision)
    deltas = lax.linalg.triangular_solve(identity + strict_part, targets, left_side=True, lower=True, unit_diagonal=True)
    end_log = cumlog[..., -1]
    weight = (jnp.exp(end_log[..., None] - cumlog) * rate_block)[..., None]
    new_state = jnp.exp(end_log)[..., None, None] * state + jnp.einsum('hcd,hcw->hdw', key_block * weight, deltas, precision=finest_precision)
    if query_block is None:
        return (new_state, None)
    query_dots = jnp.einsum('hcd,hed->hce', query_block, key_block, precision=finest_precision)
    mixing = jnp.where(row_index >= col_index, decays * query_dots * rate_block[..., None, :], 0.0)
    result = start_decay * jnp.einsum('hcd,hdw->hcw', query_block, state, precision=finest_precision)
    result = result + jnp.einsum('hce,hew->hcw', mixing, deltas, precision=finest_precision)
    return (new_state, result)

def run_blocks(query_heads, key_heads, value_heads, rate_heads, log_heads, state):
    head_count = rate_heads.shape[0]
    length = rate_heads.shape[1]
    block_count = length // BLOCK

    def to_blocks(array):
        return jnp.moveaxis(array.reshape((head_count, block_count, BLOCK) + array.shape[2:]), 1, 0)
    query_part = None if query_heads is None else to_blocks(query_heads)
    block_items = (query_part, to_blocks(key_heads), to_blocks(value_heads), to_blocks(rate_heads), to_blocks(log_heads))
    state, results = lax.scan(block_step, state, block_items)
    if results is not None:
        results = jnp.moveaxis(results, 0, 1).reshape(head_count, length, results.shape[-1])
    return (state, results)

def head_forward(query_head, key_head, value_head, rate_head, log_head, output_norm_gain):
    query_unit = unit_rows(query_head) * DK ** (-0.5)
    key_unit = unit_rows(key_head)
    zero_state = jnp.zeros((1, DK, VALUE_HEAD_SIZE), jnp.float32)
    unused, results = run_blocks(query_unit[None], key_unit[None], value_head[None], rate_head[None], log_head[None], zero_state)
    output = results[0]
    return output * lax.rsqrt(lax.optimization_barrier(jnp.mean(output * output, axis=-1, keepdims=True)) + 1e-06) * output_norm_gain

def reference(query_matrix_rows, key_matrix_rows, value_matrix_rows, write_strength, forget_gate_code, value_to_key_head, output_norm_gain, output_weight, adapter_lowering, adapter_raising, output_gradient):
    finest_precision = lax.Precision.HIGHEST
    log_gate = jnp.log1p(-forget_gate_code.astype(jnp.float32) * 2.0 ** (-20))
    gradient_single = output_gradient.astype(jnp.float32)
    projected_output = jnp.dot(output_gradient.astype(jnp.float32), output_weight.T.astype(jnp.float32), preferred_element_type=jnp.float32)
    gradient_lowrank = jnp.dot(gradient_single, adapter_raising.T, precision=finest_precision)
    gradient_normalized = projected_output + adapter_scale * jnp.dot(gradient_lowrank, adapter_lowering, precision=finest_precision)

    def per_head(head_index):
        key_index = value_to_key_head[head_index]
        key_start = (key_index * DK).astype(jnp.int32)
        value_offset = (head_index * VALUE_HEAD_SIZE).astype(jnp.int32)
        query_head = lax.dynamic_slice_in_dim(query_matrix_rows, key_start, DK, 1).astype(jnp.float32)
        key_head = lax.dynamic_slice_in_dim(key_matrix_rows, key_start, DK, 1).astype(jnp.float32)
        value_head = lax.dynamic_slice_in_dim(value_matrix_rows, value_offset, VALUE_HEAD_SIZE, 1).astype(jnp.float32)
        grad_head = lax.dynamic_slice_in_dim(gradient_normalized, value_offset, VALUE_HEAD_SIZE, 1)
        lowering_head = lax.dynamic_slice_in_dim(adapter_lowering, value_offset, VALUE_HEAD_SIZE, 1)
        log_head = log_gate[head_index]

        def run_head(query_in, key_in, value_in, rate_in):
            return head_forward(query_in, key_in, value_in, rate_in, log_head, output_norm_gain)
        normalized_output, pullback = jax.vjp(run_head, query_head, key_head, value_head, write_strength[head_index])
        query_grad, key_grad, value_grad, rate_grad = pullback(grad_head)
        lowering_piece = adapter_scale * jnp.dot(gradient_lowrank.T, normalized_output, precision=finest_precision)
        lowrank_piece = jnp.dot(normalized_output, lowering_head.T, precision=finest_precision)
        return (query_grad, key_grad, value_grad, rate_grad, lowering_piece, lowrank_piece)
    head_ids = jnp.arange(VALUE_HEADS, dtype=jnp.int32)
    query_grads, key_grads, value_grads, rate_grads, down_parts, rank_parts = lax.map(per_head, head_ids)
    key_select = (value_to_key_head[:, None] == jnp.arange(HK, dtype=jnp.int32)[None, :]).astype(jnp.float32)
    grad_query = jnp.einsum('htd,hg->tgd', query_grads, key_select, precision=finest_precision).reshape(TOKENS, HK * DK)
    grad_key = jnp.einsum('htd,hg->tgd', key_grads, key_select, precision=finest_precision).reshape(TOKENS, HK * DK)
    grad_value = jnp.moveaxis(value_grads, 0, 1).reshape(TOKENS, VALUE_HEADS * VALUE_HEAD_SIZE)
    grad_down = jnp.moveaxis(down_parts, 0, 1).reshape(ADAPTER_RANK, VALUE_HEADS * VALUE_HEAD_SIZE)
    lowrank_total = lax.optimization_barrier(jnp.sum(rank_parts, axis=0))
    raising_gradient = adapter_scale * jnp.dot(lowrank_total.T, gradient_single, precision=finest_precision)
    return (grad_query, grad_key, grad_value, rate_grads, grad_down, raising_gradient)
```

```python
import functools

import jax
import jax.numpy as jnp
from jax import lax
from jax.experimental import pallas as pl
from jax.experimental.pallas import tpu as pltpu
from jax.sharding import PartitionSpec as P

DK = 128
DV = 128
TOK = 256
HALF = 128
HEADS = 8
KEYS = 4
RANK = 16
EPS = 1e-06
F32 = jnp.float32
BF16 = jnp.bfloat16
MESH = pl.DeviceIdType.MESH

NN = (((1,), (0,)), ((), ()))
NT = (((1,), (1,)), ((), ()))
TN = (((0,), (0,)), ((), ()))


def dot(x, y, form=NN):
    return lax.dot_general(x, y, form, preferred_element_type=F32)


def split(x):
    high = x.astype(BF16)
    return high, (x - high.astype(F32)).astype(BF16)


def cat(parts, axis):
    return jnp.concatenate(parts, axis=axis)


def dot3(x, y, form=NN):
    cx, cy = form[0][0][0], form[0][1][0]
    return dot(cat([x[0], x[1], x[0]], cx), cat([y[0], y[0], y[1]], cy), form)


def dot2(x, exact, form=NN):
    cx, cy = form[0][0][0], form[0][1][0]
    return dot(cat(list(x), cx), cat([exact, exact], cy), form)


def dot2r(exact, y, form=NN):
    cx, cy = form[0][0][0], form[0][1][0]
    return dot(cat([exact, exact], cx), cat(list(y), cy), form)


def square(x, y):
    right = cat([cat([y[0], y[1]], 1), cat([y[0], jnp.zeros_like(y[1])], 1)], 0)
    both = dot(cat([x[0], x[1]], 1), right)
    return both[:, :HALF] + both[:, HALF:]


def grid_of(rows, columns):
    return (
        lax.broadcasted_iota(jnp.int32, (rows, columns), 0),
        lax.broadcasted_iota(jnp.int32, (rows, columns), 1),
    )


def inverses(blocks):
    row, col = grid_of(HALF, HALF)
    eye = jnp.where(row == col, 1.0, 0.0).astype(F32)
    pairs = ((row >> 1) == (col >> 1)) & (row > col)
    found = [eye - jnp.where(pairs, block, 0.0) for block in blocks]
    for level in range(1, 7):
        here = ((row >> (level + 1)) == (col >> (level + 1))) & ((row >> level) > (col >> level))
        halves = [split(x) for x in found]
        inner = [
            split(square(split(jnp.where(here, block, 0.0)), x))
            for block, x in zip(blocks, halves)
        ]
        found = [x - square(h, y) for x, h, y in zip(found, halves, inner)]
    return found


ROW_R, ROW_C, ROW_P, ROW_G, ROW_BG, ROW_AG, ROW_KEY = 0, 8, 16, 24, 32, 40, 48


def local_kernel(
    which,
    q_ref,
    k_ref,
    v_ref,
    rate_ref,
    code_ref,
    og_ref,
    weight_ref,
    lower_ref,
    raise_ref,
    a_ref,
    bt_ref,
    w_ref,
    u_ref,
    e_ref,
    o_ref,
    zt_ref,
    yh_ref,
    yl_ref,
    gn_ref,
    gr_ref,
    rows_ref,
    cols_ref,
    k4,
    kt4,
    q4,
    kk4,
    qk4,
):
    lane = lax.broadcasted_iota(jnp.int32, (HEADS, TOK), 1)
    gamma = 1.0 - code_ref[...].astype(F32) * 2.0 ** (-20)
    step = 1
    while step < TOK:
        gamma = gamma * jnp.where(lane >= step, pltpu.roll(gamma, step, 1), 1.0)
        step *= 2
    back = 1.0 / gamma
    ones = jnp.ones((8, DK), BF16)
    rows_ref[...] = jnp.zeros_like(rows_ref)
    for m in range(KEYS):
        at = slice(m * DK, (m + 1) * DK)
        k = k_ref[:, at]
        q = q_ref[:, at]
        k4[m] = k
        q4[m] = q
        kt4[m] = k.T
        kk4[m] = dot(k, k, NT)
        qk4[m] = dot(q, k, NT)
        kf, qf = k.astype(F32), q.astype(F32)
        ksum = dot2r(ones, split(kf * kf), NT)[0:1]
        qsum = dot2r(ones, split(qf * qf), NT)[0:1]
        rows_ref[ROW_KEY + m : ROW_KEY + m + 1, :] = lax.rsqrt(ksum + EPS)
        rows_ref[ROW_KEY + KEYS + m : ROW_KEY + KEYS + m + 1, :] = lax.rsqrt(qsum + EPS)
    rate = rate_ref[...]
    for h in range(HEADS):
        m = which[h] % KEYS
        a = rows_ref[pl.ds(ROW_KEY + m, 1), :]
        b = rows_ref[pl.ds(ROW_KEY + KEYS + m, 1), :] * DK ** (-0.5)
        g, i, r = gamma[h : h + 1], back[h : h + 1], rate[h : h + 1]
        for at, value in (
            (ROW_R, g * a),
            (ROW_C, a * r * i),
            (ROW_P, g * b),
            (ROW_G, g),
            (ROW_BG, r * i),
            (ROW_AG, a * i),
        ):
            rows_ref[at + h : at + h + 1, :] = value
    cols_ref[...] = rows_ref[...].T
    row, col = grid_of(TOK, TOK)
    srow, scol = grid_of(HALF, HALF)
    eye = jnp.where(srow == scol, 1.0, 0.0).astype(F32)

    def column(at):
        return cols_ref[:, at : at + 1]

    def line(at):
        return rows_ref[at : at + 1, :]

    group = 4
    for start in range(0, HEADS, group):
        heads = range(start, start + group)
        keys = [which[h] % KEYS for h in heads]
        blocks, corners = [], []
        for h, m in zip(heads, keys):
            strict = jnp.where(row > col, kk4[m] * column(ROW_R + h) * line(ROW_C + h), 0.0)
            blocks += [strict[:HALF, :HALF], strict[HALF:, HALF:]]
            corners.append(split(strict[HALF:, :HALF]))
        found = inverses(blocks)
        for n, (h, m) in enumerate(zip(heads, keys)):
            first, second = split(found[2 * n]), split(found[2 * n + 1])
            corner = split(-square(second, split(square(corners[n], first))))
            blank = jnp.zeros((HALF, HALF), BF16)
            t = tuple(
                cat([cat([first[i], blank], 1), cat([corner[i], second[i]], 1)], 0)
                for i in range(2)
            )
            k, q = k4[m].astype(F32), q4[m].astype(F32)
            v = v_ref[:, h * DV : (h + 1) * DV]
            last = rows_ref[ROW_G + h : ROW_G + h + 1, TOK - 1 : TOK]
            ended = split(kt4[m].astype(F32) * (line(ROW_C + h) * last))
            zt = dot3(ended, t)
            zs = split(zt)
            scaled = k * column(ROW_R + h)
            g = split(scaled)
            zt_ref[h] = zt
            a_ref[h] = last * eye - dot3(zs, g)
            bt_ref[h] = dot2r(v.T, zs, NT)
            pair = cat([g[0], v], 1)
            wu = dot2(t, pair)
            w_ref[h] = wu[:, :DK] + dot(t[0], g[1])
            u_ref[h] = wu[:, DK:]
            mixing = jnp.where(row >= col, qk4[m] * column(ROW_P + h) * line(ROW_C + h), 0.0)
            y = split(dot3(split(mixing), t))
            yh_ref[h] = y[0]
            yl_ref[h] = y[1]
            eo = dot2(y, pair)
            e_ref[h] = q * column(ROW_P + h) - (eo[:, :DK] + dot(y[0], g[1]))
            o_ref[h] = eo[:, DK:]
    rs = split(raise_ref[...])
    both = dot(cat(list(rs), 0), og_ref[...], NT)
    grt = both[:RANK] + both[RANK:]
    gr_ref[...] = grt
    gs = split(2.0 * grt)
    for h in range(HEADS):
        at = slice(h * DV, (h + 1) * DV)
        low = dot3(gs, split(lower_ref[:, at]), TN)
        gn_ref[:, at] = dot(og_ref[...], weight_ref[at, :], NT) + low


def middle_kernel(
    which,
    s0_ref,
    q_ref,
    k_ref,
    w_ref,
    u_ref,
    e_ref,
    o_ref,
    yh_ref,
    yl_ref,
    gn_ref,
    gr_ref,
    rows_ref,
    cols_ref,
    gain_ref,
    og_ref,
    lower_ref,
    ct_ref,
    xt_ref,
    uf_ref,
    ft_ref,
    dq_ref,
    down_ref,
    raise_ref,
    k4,
    q4,
    qt4,
    acc4,
):
    for m in range(KEYS):
        at = slice(m * DK, (m + 1) * DK)
        k4[m] = k_ref[:, at]
        q4[m] = q_ref[:, at]
        qt4[m] = q_ref[:, at].T
    acc4[...] = jnp.zeros_like(acc4)
    row, col = grid_of(TOK, TOK)
    gain = gain_ref[...]
    gs = split(2.0 * gr_ref[...])
    rank = jnp.zeros((RANK, TOK), F32)
    for h in range(HEADS):
        m = which[h] % KEYS
        at = slice(h * DV, (h + 1) * DV)
        ss = split(s0_ref[h])
        es = split(e_ref[h])
        ws = split(w_ref[h])
        o = o_ref[h] + dot3(es, ss, NT)
        u = u_ref[h] - dot3(ws, ss, NT)
        uf_ref[h] = u
        r = lax.rsqrt(jnp.mean(o * o, axis=-1, keepdims=True) + EPS)
        gn = gn_ref[:, at] * gain
        tail = jnp.mean(gn * o, axis=-1, keepdims=True)
        do = r * gn - o * (r * r * r * tail)
        normed = split(o * r * gain)
        dts = split(do.T)
        ct_ref[h] = dot3(dts, es)
        xt_ref[h] = dot3(dts, (yh_ref[h], yl_ref[h]))
        rank = rank + dot3(split(lower_ref[:, at]), normed, NT)
        down_ref[:, at] = dot3(gs, normed)
        ds, us = split(do), split(u)
        dp = split(jnp.where(row >= col, dot3(ds, us, NT), 0.0))
        ck = split(k4[m].astype(F32) * cols_ref[:, ROW_C + h : ROW_C + h + 1])
        dqh = (dot3(ds, ss) + dot3(dp, ck)) * cols_ref[:, ROW_G + h : ROW_G + h + 1]
        pq = split(qt4[m].astype(F32) * rows_ref[ROW_P + h : ROW_P + h + 1, :])
        ft_ref[h] = dot3(pq, dp)
        acc4[m] = acc4[m] + dqh
    raise_ref[...] = 2.0 * dot2(split(rank), og_ref[...])
    for m in range(KEYS):
        total = acc4[m]
        q = q4[m].astype(F32)
        inv = cols_ref[:, ROW_KEY + KEYS + m : ROW_KEY + KEYS + m + 1]
        along = jnp.sum(total * q, axis=-1, keepdims=True)
        dq_ref[:, m * DK : (m + 1) * DK] = (DK ** (-0.5) * inv) * (total - q * (inv * inv * along))


def last_kernel(
    which,
    ds_ref,
    s0_ref,
    k_ref,
    xt_ref,
    zt_ref,
    u_ref,
    ft_ref,
    rows_ref,
    cols_ref,
    dk_ref,
    dv_ref,
    db_ref,
    k4,
    kt4,
    acc4,
    acct4,
):
    for m in range(KEYS):
        at = slice(m * DK, (m + 1) * DK)
        k4[m] = k_ref[:, at]
        kt4[m] = k_ref[:, at].T
    acc4[...] = jnp.zeros_like(acc4)
    acct4[...] = jnp.zeros_like(acct4)
    row, col = grid_of(TOK, TOK)
    for h in range(HEADS):
        m = which[h] % KEYS
        dst = ds_ref[h]
        drt = xt_ref[h] + dot3(split(dst), split(zt_ref[h]))
        dr = drt.T
        dv_ref[:, h * DV : (h + 1) * DV] = dr
        drs, us = split(dr), split(u_ref[h])
        dl = split(jnp.where(row > col, -dot3(drs, us, NT), 0.0))
        kt = kt4[m].astype(F32)
        rk = split(kt * rows_ref[ROW_R + h : ROW_R + h + 1, :])
        ck = split(k4[m].astype(F32) * cols_ref[:, ROW_C + h : ROW_C + h + 1])
        last = rows_ref[ROW_G + h : ROW_G + h + 1, TOK - 1 : TOK]
        f = ft_ref[h] + dot3(rk, dl) + last * dot3(split(dst.T), us, NT)
        db_ref[h : h + 1, :] = (
            jnp.sum(kt * f, axis=0, keepdims=True) * rows_ref[ROW_AG + h : ROW_AG + h + 1, :]
        )
        own = dot3(dl, ck) - dot3(drs, split(s0_ref[h]))
        acc4[m] = acc4[m] + own * cols_ref[:, ROW_G + h : ROW_G + h + 1]
        acct4[m] = acct4[m] + f * rows_ref[ROW_BG + h : ROW_BG + h + 1, :]
    for m in range(KEYS):
        total = acc4[m] + acct4[m].T
        k = k4[m].astype(F32)
        inv = cols_ref[:, ROW_KEY + m : ROW_KEY + m + 1]
        along = jnp.sum(total * k, axis=-1, keepdims=True)
        dk_ref[:, m * DK : (m + 1) * DK] = inv * (total - k * (inv * inv * along))


def greet(count, me):
    barrier = pltpu.get_barrier_semaphore()

    def one(s, carry):
        other = lax.rem(me + s, count)
        pl.semaphore_signal(barrier, inc=1, device_id={"seq": other}, device_id_type=MESH)
        return carry

    lax.fori_loop(1, count, one, 0)
    pl.semaphore_wait(barrier, count - 1)


def scan_kernel(count, backward, *refs):
    if backward:
        b_ref, all_ref, s_ref, bbuf, sbuf, send_sem, b_sem, s_sem = refs
    else:
        a_ref, b_ref, s_ref, all_ref, bbuf, sbuf, send_sem, b_sem, s_sem, a_sem, asend_sem = refs
    me = lax.axis_index("seq")
    rows = HEADS * DV // count
    per = DV // rows

    def piece(ref, owner):
        head = owner // per
        return ref.at[head, pl.ds(pl.multiple_of(lax.rem(owner, per) * rows, rows), rows)]

    def remote(src, dst, ssem, rsem, other):
        return pltpu.make_async_remote_copy(
            src_ref=src,
            dst_ref=dst,
            send_sem=ssem,
            recv_sem=rsem,
            device_id={"seq": other},
            device_id_type=MESH,
        )

    def arrived(ref, sem):
        pltpu.make_async_copy(ref, ref, sem).wait()

    own_b = pltpu.make_async_copy(piece(b_ref, me), bbuf.at[me], b_sem.at[me])
    own_b.start()
    if not backward:
        own_a = pltpu.make_async_copy(a_ref.at[me // per], all_ref.at[me], a_sem.at[me])
        own_a.start()
    greet(count, me)

    def deal(s, carry):
        other = lax.rem(me + s, count)
        if not backward:
            remote(
                a_ref.at[other // per], all_ref.at[me], asend_sem.at[other], a_sem.at[me], other
            ).start()
        remote(
            piece(b_ref, other), bbuf.at[me], send_sem.at[other], b_sem.at[me], other
        ).start()
        return carry

    lax.fori_loop(1, count, deal, 0)

    sbuf[0] = jnp.zeros((rows, DK), F32)

    def turn(t, carry):
        j = count - 1 - t if backward else t

        @pl.when(j == me)
        def _():
            pltpu.make_async_copy(sbuf.at[t], piece(s_ref, me), s_sem.at[me]).start()

        @pl.when(j != me)
        def _():
            remote(
                sbuf.at[t], piece(s_ref, me), send_sem.at[count + j], s_sem.at[me], j
            ).start()

        arrived(bbuf.at[j], b_sem.at[j])
        if not backward:
            arrived(all_ref.at[j], a_sem.at[j])
        form = NN if backward else NT
        sbuf[t + 1] = dot3(split(sbuf[t]), split(all_ref[j]), form) + bbuf[j]
        return carry

    lax.fori_loop(0, count, turn, 0)

    def settle(s, carry):
        other = lax.rem(me + s, count)
        arrived(piece(b_ref, other), send_sem.at[other])
        arrived(sbuf.at[other], send_sem.at[count + other])
        if not backward:
            arrived(a_ref.at[other // per], asend_sem.at[other])
        arrived(piece(s_ref, other), s_sem.at[other])
        return carry

    lax.fori_loop(1, count, settle, 0)
    arrived(piece(s_ref, me), s_sem.at[me])


VM = pl.BlockSpec(memory_space=pltpu.VMEM)
SM = pl.BlockSpec(memory_space=pltpu.SMEM)
LIMIT = 56 * 1024 * 1024


def struct(*shape, dtype=F32):
    return jax.ShapeDtypeStruct(shape, dtype)


def forward_scan(a, bt, count):
    rows = HEADS * DV // count
    return pl.pallas_call(
        functools.partial(scan_kernel, count, False),
        out_shape=(struct(HEADS, DV, DK), struct(count, DK, DK)),
        in_specs=[VM] * 2,
        out_specs=(VM, VM),
        scratch_shapes=[
            pltpu.VMEM((count, rows, DK), F32),
            pltpu.VMEM((count + 1, rows, DK), F32),
            pltpu.SemaphoreType.DMA((2 * count,)),
            pltpu.SemaphoreType.DMA((count,)),
            pltpu.SemaphoreType.DMA((count,)),
            pltpu.SemaphoreType.DMA((count,)),
            pltpu.SemaphoreType.DMA((count,)),
        ],
        compiler_params=pltpu.CompilerParams(
            collective_id=0, has_side_effects=True, vmem_limit_bytes=LIMIT
        ),
        name="forward_states",
    )(a, bt)


def backward_scan(ct, everyone, count):
    rows = HEADS * DV // count
    return pl.pallas_call(
        functools.partial(scan_kernel, count, True),
        out_shape=struct(HEADS, DV, DK),
        in_specs=[VM] * 2,
        out_specs=VM,
        scratch_shapes=[
            pltpu.VMEM((count, rows, DK), F32),
            pltpu.VMEM((count + 1, rows, DK), F32),
            pltpu.SemaphoreType.DMA((2 * count,)),
            pltpu.SemaphoreType.DMA((count,)),
            pltpu.SemaphoreType.DMA((count,)),
        ],
        compiler_params=pltpu.CompilerParams(
            collective_id=1, has_side_effects=True, vmem_limit_bytes=LIMIT
        ),
        name="state_gradients",
    )(ct, everyone)


def body(
    query_matrix_rows,
    key_matrix_rows,
    value_matrix_rows,
    write_strength,
    forget_gate_code,
    value_to_key_head,
    output_norm_gain,
    output_weight,
    adapter_lowering,
    adapter_raising,
    output_gradient,
):
    count = lax.axis_size("seq")
    params = pltpu.CompilerParams(vmem_limit_bytes=LIMIT)
    per_head = struct(HEADS, TOK, DK)
    a, bt, w, u, e, o, zt, yh, yl, gn, gr, rows, cols = pl.pallas_call(
        local_kernel,
        out_shape=(
            struct(HEADS, DK, DK),
            struct(HEADS, DV, DK),
            per_head,
            per_head,
            per_head,
            per_head,
            struct(HEADS, DK, TOK),
            struct(HEADS, TOK, TOK, dtype=BF16),
            struct(HEADS, TOK, TOK, dtype=BF16),
            struct(TOK, HEADS * DV),
            struct(RANK, TOK),
            struct(128, TOK),
            struct(TOK, 128),
        ),
        in_specs=[SM] + [VM] * 9,
        out_specs=(VM,) * 13,
        scratch_shapes=[
            pltpu.VMEM((KEYS, TOK, DK), BF16),
            pltpu.VMEM((KEYS, DK, TOK), BF16),
            pltpu.VMEM((KEYS, TOK, DK), BF16),
            pltpu.VMEM((KEYS, TOK, TOK), F32),
            pltpu.VMEM((KEYS, TOK, TOK), F32),
        ],
        compiler_params=params,
        name="local_pass",
    )(
        value_to_key_head,
        query_matrix_rows,
        key_matrix_rows,
        value_matrix_rows,
        write_strength,
        forget_gate_code,
        output_gradient,
        output_weight,
        adapter_lowering,
        adapter_raising,
    )
    s0, everyone = forward_scan(a, bt, count)
    ct, xt, uf, ft, dq, down, lift = pl.pallas_call(
        middle_kernel,
        out_shape=(
            struct(HEADS, DV, DK),
            struct(HEADS, DV, TOK),
            per_head,
            struct(HEADS, DK, TOK),
            struct(TOK, KEYS * DK),
            struct(RANK, HEADS * DV),
            struct(RANK, output_gradient.shape[1]),
        ),
        in_specs=[SM] + [VM] * 16,
        out_specs=(VM,) * 7,
        scratch_shapes=[
            pltpu.VMEM((KEYS, TOK, DK), BF16),
            pltpu.VMEM((KEYS, TOK, DK), BF16),
            pltpu.VMEM((KEYS, DK, TOK), BF16),
            pltpu.VMEM((KEYS, TOK, DK), F32),
        ],
        compiler_params=params,
        name="middle_pass",
    )(
        value_to_key_head,
        s0,
        query_matrix_rows,
        key_matrix_rows,
        w,
        u,
        e,
        o,
        yh,
        yl,
        gn,
        gr,
        rows,
        cols,
        output_norm_gain.reshape(1, DV),
        output_gradient,
        adapter_lowering,
    )
    grad_down = lax.psum(down, "seq")
    raising_gradient = lax.psum(lift, ("seq", "head"))
    ds = backward_scan(ct, everyone, count)
    dk, dv, db = pl.pallas_call(
        last_kernel,
        out_shape=(
            struct(TOK, KEYS * DK),
            struct(TOK, HEADS * DV),
            struct(HEADS, TOK),
        ),
        in_specs=[SM] + [VM] * 9,
        out_specs=(VM,) * 3,
        scratch_shapes=[
            pltpu.VMEM((KEYS, TOK, DK), BF16),
            pltpu.VMEM((KEYS, DK, TOK), BF16),
            pltpu.VMEM((KEYS, TOK, DK), F32),
            pltpu.VMEM((KEYS, DK, TOK), F32),
        ],
        compiler_params=params,
        name="last_pass",
    )(value_to_key_head, ds, s0, key_matrix_rows, xt, zt, uf, ft, rows, cols)
    return (dq, dk, dv, db, grad_down, raising_gradient)


def solution(mesh):
    placed = (
        P("seq", "head"),
        P("seq", "head"),
        P("seq", "head"),
        P("head", "seq"),
        P("head", "seq"),
        P("head"),
        P(),
        P("head", None),
        P(None, "head"),
        P(),
        P("seq", None),
    )
    return jax.shard_map(
        body,
        mesh=mesh,
        in_specs=placed,
        out_specs=(
            P("seq", "head"),
            P("seq", "head"),
            P("seq", "head"),
            P("head", "seq"),
            P(None, "head"),
            P(),
        ),
        check_vma=False,
    )
```

```python
import functools

import jax
import jax.numpy as jnp
from jax import lax
from jax.experimental import pallas as pl
from jax.experimental.pallas import tpu as pltpu
from jax.sharding import PartitionSpec as P

DK = 128
DV = 128
TOK = 256
HALF = 128
HEADS = 8
KEYS = 4
RANK = 16
EPS = 1e-06
F32 = jnp.float32
BF16 = jnp.bfloat16
MESH = pl.DeviceIdType.MESH

NN = (((1,), (0,)), ((), ()))
NT = (((1,), (1,)), ((), ()))
TN = (((0,), (0,)), ((), ()))


def dot(x, y, form=NN):
    return lax.dot_general(x, y, form, preferred_element_type=F32)


def split(x):
    high = x.astype(BF16)
    return high, (x - high.astype(F32)).astype(BF16)


def cat(parts, axis):
    return jnp.concatenate(parts, axis=axis)


def dot3(x, y, form=NN):
    cx, cy = form[0][0][0], form[0][1][0]
    return dot(cat([x[0], x[1], x[0]], cx), cat([y[0], y[0], y[1]], cy), form)


def dot2(x, exact, form=NN):
    cx, cy = form[0][0][0], form[0][1][0]
    return dot(cat(list(x), cx), cat([exact, exact], cy), form)


def dot2r(exact, y, form=NN):
    cx, cy = form[0][0][0], form[0][1][0]
    return dot(cat([exact, exact], cx), cat(list(y), cy), form)


def square(x, y):
    right = cat([cat([y[0], y[1]], 1), cat([y[0], jnp.zeros_like(y[1])], 1)], 0)
    both = dot(cat([x[0], x[1]], 1), right)
    return both[:, :HALF] + both[:, HALF:]


def grid_of(rows, columns):
    return (
        lax.broadcasted_iota(jnp.int32, (rows, columns), 0),
        lax.broadcasted_iota(jnp.int32, (rows, columns), 1),
    )


def inverses(blocks):
    row, col = grid_of(HALF, HALF)
    eye = jnp.where(row == col, 1.0, 0.0).astype(F32)
    pairs = ((row >> 1) == (col >> 1)) & (row > col)
    found = [eye - jnp.where(pairs, block, 0.0) for block in blocks]
    for level in range(1, 7):
        here = ((row >> (level + 1)) == (col >> (level + 1))) & ((row >> level) > (col >> level))
        halves = [split(x) for x in found]
        inner = [
            split(square(split(jnp.where(here, block, 0.0)), x))
            for block, x in zip(blocks, halves)
        ]
        found = [x - square(h, y) for x, h, y in zip(found, halves, inner)]
    return found


ROW_R, ROW_C, ROW_P, ROW_G, ROW_BG, ROW_AG, ROW_KEY = 0, 8, 16, 24, 32, 40, 48


def local_kernel(
    which,
    q_ref,
    k_ref,
    v_ref,
    rate_ref,
    code_ref,
    og_ref,
    weight_ref,
    lower_ref,
    raise_ref,
    a_ref,
    bt_ref,
    w_ref,
    u_ref,
    e_ref,
    o_ref,
    zt_ref,
    yh_ref,
    yl_ref,
    gn_ref,
    gr_ref,
    rows_ref,
    cols_ref,
    k4,
    kt4,
    q4,
    kk4,
    qk4,
):
    lane = lax.broadcasted_iota(jnp.int32, (HEADS, TOK), 1)
    gamma = 1.0 - code_ref[...].astype(F32) * 2.0 ** (-20)
    step = 1
    while step < TOK:
        gamma = gamma * jnp.where(lane >= step, pltpu.roll(gamma, step, 1), 1.0)
        step *= 2
    back = 1.0 / gamma
    ones = jnp.ones((8, DK), BF16)
    rows_ref[...] = jnp.zeros_like(rows_ref)
    for m in range(KEYS):
        at = slice(m * DK, (m + 1) * DK)
        k = k_ref[:, at]
        q = q_ref[:, at]
        k4[m] = k
        q4[m] = q
        kt4[m] = k.T
        kk4[m] = dot(k, k, NT)
        qk4[m] = dot(q, k, NT)
        kf, qf = k.astype(F32), q.astype(F32)
        ksum = dot2r(ones, split(kf * kf), NT)[0:1]
        qsum = dot2r(ones, split(qf * qf), NT)[0:1]
        rows_ref[ROW_KEY + m : ROW_KEY + m + 1, :] = lax.rsqrt(ksum + EPS)
        rows_ref[ROW_KEY + KEYS + m : ROW_KEY + KEYS + m + 1, :] = lax.rsqrt(qsum + EPS)
    rate = rate_ref[...]
    for h in range(HEADS):
        m = which[h] % KEYS
        a = rows_ref[pl.ds(ROW_KEY + m, 1), :]
        b = rows_ref[pl.ds(ROW_KEY + KEYS + m, 1), :] * DK ** (-0.5)
        g, i, r = gamma[h : h + 1], back[h : h + 1], rate[h : h + 1]
        for at, value in (
            (ROW_R, g * a),
            (ROW_C, a * r * i),
            (ROW_P, g * b),
            (ROW_G, g),
            (ROW_BG, r * i),
            (ROW_AG, a * i),
        ):
            rows_ref[at + h : at + h + 1, :] = value
    cols_ref[...] = rows_ref[...].T
    row, col = grid_of(TOK, TOK)
    srow, scol = grid_of(HALF, HALF)
    eye = jnp.where(srow == scol, 1.0, 0.0).astype(F32)

    def column(at):
        return cols_ref[:, at : at + 1]

    def line(at):
        return rows_ref[at : at + 1, :]

    group = 4
    for start in range(0, HEADS, group):
        heads = range(start, start + group)
        keys = [which[h] % KEYS for h in heads]
        blocks, corners = [], []
        for h, m in zip(heads, keys):
            strict = jnp.where(row > col, kk4[m] * column(ROW_R + h) * line(ROW_C + h), 0.0)
            blocks += [strict[:HALF, :HALF], strict[HALF:, HALF:]]
            corners.append(split(strict[HALF:, :HALF]))
        found = inverses(blocks)
        for n, (h, m) in enumerate(zip(heads, keys)):
            first, second = split(found[2 * n]), split(found[2 * n + 1])
            corner = split(-square(second, split(square(corners[n], first))))
            blank = jnp.zeros((HALF, HALF), BF16)
            t = tuple(
                cat([cat([first[i], blank], 1), cat([corner[i], second[i]], 1)], 0)
                for i in range(2)
            )
            k, q = k4[m].astype(F32), q4[m].astype(F32)
            v = v_ref[:, h * DV : (h + 1) * DV]
            last = rows_ref[ROW_G + h : ROW_G + h + 1, TOK - 1 : TOK]
            ended = split(kt4[m].astype(F32) * (line(ROW_C + h) * last))
            zt = dot3(ended, t)
            zs = split(zt)
            scaled = k * column(ROW_R + h)
            g = split(scaled)
            zt_ref[h] = zt
            a_ref[h] = last * eye - dot3(zs, g)
            bt_ref[h] = dot2r(v.T, zs, NT)
            pair = cat([g[0], v], 1)
            wu = dot2(t, pair)
            w_ref[h] = wu[:, :DK] + dot(t[0], g[1])
            u_ref[h] = wu[:, DK:]
            mixing = jnp.where(row >= col, qk4[m] * column(ROW_P + h) * line(ROW_C + h), 0.0)
            y = split(dot3(split(mixing), t))
            yh_ref[h] = y[0]
            yl_ref[h] = y[1]
            eo = dot2(y, pair)
            e_ref[h] = q * column(ROW_P + h) - (eo[:, :DK] + dot(y[0], g[1]))
            o_ref[h] = eo[:, DK:]
    rs = split(raise_ref[...])
    both = dot(cat(list(rs), 0), og_ref[...], NT)
    grt = both[:RANK] + both[RANK:]
    gr_ref[...] = grt
    gs = split(2.0 * grt)
    for h in range(HEADS):
        at = slice(h * DV, (h + 1) * DV)
        low = dot3(gs, split(lower_ref[:, at]), TN)
        gn_ref[:, at] = dot(og_ref[...], weight_ref[at, :], NT) + low


def middle_kernel(
    which,
    s0_ref,
    q_ref,
    k_ref,
    w_ref,
    u_ref,
    e_ref,
    o_ref,
    yh_ref,
    yl_ref,
    gn_ref,
    gr_ref,
    rows_ref,
    cols_ref,
    gain_ref,
    og_ref,
    lower_ref,
    ct_ref,
    xt_ref,
    uf_ref,
    ft_ref,
    dq_ref,
    red_ref,
    k4,
    q4,
    qt4,
    acc4,
):
    for m in range(KEYS):
        at = slice(m * DK, (m + 1) * DK)
        k4[m] = k_ref[:, at]
        q4[m] = q_ref[:, at]
        qt4[m] = q_ref[:, at].T
    acc4[...] = jnp.zeros_like(acc4)
    row, col = grid_of(TOK, TOK)
    gain = gain_ref[...]
    gs = split(2.0 * gr_ref[...])
    rank = jnp.zeros((RANK, TOK), F32)
    for h in range(HEADS):
        m = which[h] % KEYS
        at = slice(h * DV, (h + 1) * DV)
        ss = split(s0_ref[h])
        es = split(e_ref[h])
        ws = split(w_ref[h])
        o = o_ref[h] + dot3(es, ss, NT)
        u = u_ref[h] - dot3(ws, ss, NT)
        uf_ref[h] = u
        r = lax.rsqrt(jnp.mean(o * o, axis=-1, keepdims=True) + EPS)
        gn = gn_ref[:, at] * gain
        tail = jnp.mean(gn * o, axis=-1, keepdims=True)
        do = r * gn - o * (r * r * r * tail)
        normed = split(o * r * gain)
        dts = split(do.T)
        ct_ref[h] = dot3(dts, es)
        xt_ref[h] = dot3(dts, (yh_ref[h], yl_ref[h]))
        rank = rank + dot3(split(lower_ref[:, at]), normed, NT)
        red_ref[h] = dot3(gs, normed)
        ds, us = split(do), split(u)
        dp = split(jnp.where(row >= col, dot3(ds, us, NT), 0.0))
        ck = split(k4[m].astype(F32) * cols_ref[:, ROW_C + h : ROW_C + h + 1])
        dqh = (dot3(ds, ss) + dot3(dp, ck)) * cols_ref[:, ROW_G + h : ROW_G + h + 1]
        pq = split(qt4[m].astype(F32) * rows_ref[ROW_P + h : ROW_P + h + 1, :])
        ft_ref[h] = dot3(pq, dp)
        acc4[m] = acc4[m] + dqh
    lift = 2.0 * dot2(split(rank), og_ref[...])
    for n in range(lift.shape[1] // 128):
        red_ref[HEADS + n] = lift[:, n * 128 : (n + 1) * 128]
    for m in range(KEYS):
        total = acc4[m]
        q = q4[m].astype(F32)
        inv = cols_ref[:, ROW_KEY + KEYS + m : ROW_KEY + KEYS + m + 1]
        along = jnp.sum(total * q, axis=-1, keepdims=True)
        dq_ref[:, m * DK : (m + 1) * DK] = (DK ** (-0.5) * inv) * (total - q * (inv * inv * along))


def last_kernel(
    which,
    ds_ref,
    s0_ref,
    k_ref,
    xt_ref,
    zt_ref,
    u_ref,
    ft_ref,
    rows_ref,
    cols_ref,
    fin_ref,
    dk_ref,
    dv_ref,
    db_ref,
    down_ref,
    raise_ref,
    k4,
    kt4,
    acc4,
    acct4,
):
    for m in range(KEYS):
        at = slice(m * DK, (m + 1) * DK)
        k4[m] = k_ref[:, at]
        kt4[m] = k_ref[:, at].T
    acc4[...] = jnp.zeros_like(acc4)
    acct4[...] = jnp.zeros_like(acct4)
    for n in range(HEADS):
        down_ref[:, n * 128 : (n + 1) * 128] = fin_ref[n]
    for n in range(raise_ref.shape[1] // 128):
        raise_ref[:, n * 128 : (n + 1) * 128] = fin_ref[HEADS + n]
    row, col = grid_of(TOK, TOK)
    for h in range(HEADS):
        m = which[h] % KEYS
        dst = ds_ref[h]
        drt = xt_ref[h] + dot3(split(dst), split(zt_ref[h]))
        dr = drt.T
        dv_ref[:, h * DV : (h + 1) * DV] = dr
        drs, us = split(dr), split(u_ref[h])
        dl = split(jnp.where(row > col, -dot3(drs, us, NT), 0.0))
        kt = kt4[m].astype(F32)
        rk = split(kt * rows_ref[ROW_R + h : ROW_R + h + 1, :])
        ck = split(k4[m].astype(F32) * cols_ref[:, ROW_C + h : ROW_C + h + 1])
        last = rows_ref[ROW_G + h : ROW_G + h + 1, TOK - 1 : TOK]
        f = ft_ref[h] + dot3(rk, dl) + last * dot3(split(dst.T), us, NT)
        db_ref[h : h + 1, :] = (
            jnp.sum(kt * f, axis=0, keepdims=True) * rows_ref[ROW_AG + h : ROW_AG + h + 1, :]
        )
        own = dot3(dl, ck) - dot3(drs, split(s0_ref[h]))
        acc4[m] = acc4[m] + own * cols_ref[:, ROW_G + h : ROW_G + h + 1]
        acct4[m] = acct4[m] + f * rows_ref[ROW_BG + h : ROW_BG + h + 1, :]
    for m in range(KEYS):
        total = acc4[m] + acct4[m].T
        k = k4[m].astype(F32)
        inv = cols_ref[:, ROW_KEY + m : ROW_KEY + m + 1]
        along = jnp.sum(total * k, axis=-1, keepdims=True)
        dk_ref[:, m * DK : (m + 1) * DK] = inv * (total - k * (inv * inv * along))


def remote(src, dst, ssem, rsem, **where):
    return pltpu.make_async_remote_copy(
        src_ref=src,
        dst_ref=dst,
        send_sem=ssem,
        recv_sem=rsem,
        device_id=where,
        device_id_type=MESH,
    )


def arrived(ref, sem):
    pltpu.make_async_copy(ref, ref, sem).wait()


def greet(count, me, step, extra=()):
    barrier = pltpu.get_barrier_semaphore()

    def one(s, carry):
        other = lax.rem(me + s * step, count)
        pl.semaphore_signal(barrier, inc=1, device_id={"seq": other}, device_id_type=MESH)
        return carry

    lax.fori_loop(1, count // step, one, 0)
    for where in extra:
        pl.semaphore_signal(barrier, inc=1, device_id=where, device_id_type=MESH)
    pl.semaphore_wait(barrier, count // step - 1 + len(extra))


OWN = HEADS // 2


def place(count):
    me = lax.axis_index("seq")
    core = lax.rem(me, 2)
    return me, me // 2, core, me + 1 - 2 * core


def piece(ref, owner, rows):
    per = DV // rows
    return ref.at[owner // per, pl.ds(pl.multiple_of(lax.rem(owner, per) * rows, rows), rows)]


def deliver(chips, chip, core, rows, sbuf, gin, send_sem, in_sem, slots):
    for slot, j in slots:

        @pl.when(chip == j)
        def _():
            pltpu.make_async_copy(sbuf.at[slot], piece(gin, chip, rows), in_sem.at[chip]).start()

        @pl.when(chip != j)
        def _():
            remote(
                sbuf.at[slot],
                piece(gin, chip, rows),
                send_sem.at[j],
                in_sem.at[chip],
                seq=2 * j + core,
            ).start()


def forward_kernel(count, *refs):
    (
        a_ref, b_ref, s_ref, ah_ref, al_ref, first_ref, second_ref,
        siba, sibb, comb, combb, firstb, abuf, bbuf, sbuf, gin, stage,
        pair_a, pair_b, pair_as, pair_bs, deal_a, deal_b, in_a, in_b, send_sem, in_sem, fix_s, fix_r,
    ) = refs
    chips = count // 2
    rows = OWN * DV // chips
    me, chip, core, sibling = place(count)
    mine, theirs = core * OWN, (1 - core) * OWN
    greet(count, me, 2, ({"seq": sibling},))
    for n in range(OWN):
        remote(a_ref.at[theirs + n], siba.at[n], pair_as.at[n], pair_a.at[n], seq=sibling).start()
        remote(b_ref.at[theirs + n], sibb.at[n], pair_bs.at[n], pair_b.at[n], seq=sibling).start()
    lead = core == 0
    per = DV // rows
    for n in range(OWN):
        arrived(siba.at[n], pair_a.at[n])
        arrived(sibb.at[n], pair_b.at[n])
        oa, ob, ta, tb = a_ref[mine + n], b_ref[mine + n], siba[n], sibb[n]
        first, second = jnp.where(lead, oa, ta), jnp.where(lead, ta, oa)
        fb, sb = jnp.where(lead, ob, tb), jnp.where(lead, tb, ob)
        first_ref[n] = first
        second_ref[n] = second
        firstb[n] = fb
        ss = split(second)
        comb[n] = dot3(ss, split(first))
        combb[n] = dot3(split(fb), ss, NT) + sb
        for p in range(per):
            owner = n * per + p

            @pl.when(chip == owner)
            def _():
                pltpu.make_async_copy(comb.at[n], abuf.at[chip], in_a.at[chip]).start()
                pltpu.make_async_copy(
                    piece(combb, owner, rows), bbuf.at[chip], in_b.at[chip]
                ).start()

            @pl.when(chip != owner)
            def _():
                there = 2 * owner + core
                remote(
                    comb.at[n], abuf.at[chip], deal_a.at[owner], in_a.at[chip], seq=there
                ).start()
                remote(
                    piece(combb, owner, rows),
                    bbuf.at[chip],
                    deal_b.at[owner],
                    in_b.at[chip],
                    seq=there,
                ).start()

    def take(j, carry):
        arrived(abuf.at[j], in_a.at[j])
        high, low = split(abuf[j])
        ah_ref[j] = high
        al_ref[j] = low
        arrived(bbuf.at[j], in_b.at[j])
        return carry

    lax.fori_loop(0, chips, take, 0)
    state = jnp.zeros((rows, DK), F32)
    batch = max(1, chips // 2)
    for start in range(0, chips, batch):
        for j in range(start, start + batch):
            sbuf[j] = state
            state = dot3(split(state), (ah_ref[j], al_ref[j]), NT) + bbuf[j]
        deliver(
            chips, chip, core, rows, sbuf, gin, send_sem, in_sem,
            [(j, j) for j in range(start, start + batch)],
        )

    for n in range(OWN):
        for p in range(per):
            arrived(piece(gin, n * per + p, rows), in_sem.at[n * per + p])
        entering = gin[n]
        between = dot3(split(entering), split(first_ref[n]), NT) + firstb[n]
        s_ref[mine + n] = jnp.where(lead, entering, between)
        stage[n] = jnp.where(lead, between, entering)
        remote(stage.at[n], s_ref.at[mine + n], fix_s.at[n], fix_r.at[n], seq=sibling).start()
    for n in range(OWN):
        arrived(siba.at[n], pair_as.at[n])
        arrived(sibb.at[n], pair_bs.at[n])
        arrived(stage.at[n], fix_s.at[n])
        arrived(s_ref.at[theirs + n], fix_r.at[n])

    def settle(s, carry):
        other = lax.rem(chip + s, chips)
        arrived(abuf.at[other], deal_a.at[other])
        arrived(bbuf.at[other], deal_b.at[other])
        arrived(sbuf.at[other], send_sem.at[other])
        return carry

    lax.fori_loop(1, chips, settle, 0)


def backward_kernel(count, heads, blocks, *refs):
    (
        c_ref, ah_ref, al_ref, first_ref, second_ref, red_ref, s_ref, fin_ref,
        sibc, combc, secondc, bbuf, sbuf, gin, stage, gather, zbuf,
        pair_r, pair_s, deal_s, in_b, send_sem, in_sem, fix_s, fix_r,
        red_s, red_r, z_s, z_r, fin_s, fin_r,
    ) = refs
    chips = count // 2
    rows = OWN * DV // chips
    me, chip, core, sibling = place(count)
    mine, theirs = core * OWN, (1 - core) * OWN
    line = lax.axis_index("head")
    share = -(-blocks // count)
    owners = -(-blocks // share)
    peers = [lax.rem(line + s, heads) for s in range(1, heads)]
    greet(count, me, 1, tuple({"head": peer} for peer in peers))
    for n in range(OWN):
        remote(c_ref.at[theirs + n], sibc.at[n], pair_s.at[n], pair_r.at[n], seq=sibling).start()

    def scatter(o, carry):
        @pl.when(o != me)
        def _():
            remote(
                red_ref.at[pl.ds(o * share, share)],
                gather.at[me],
                red_s.at[o],
                red_r.at[me],
                seq=o,
            ).start()

        return carry

    lead = core == 0
    per = DV // rows
    for n in range(OWN):
        arrived(sibc.at[n], pair_r.at[n])
        oc, tc = c_ref[mine + n], sibc[n]
        first, second = jnp.where(lead, oc, tc), jnp.where(lead, tc, oc)
        secondc[n] = second
        combc[n] = dot3(split(second), split(first_ref[n])) + first
        for p in range(per):
            owner = n * per + p

            @pl.when(chip == owner)
            def _():
                pltpu.make_async_copy(
                    piece(combc, owner, rows), bbuf.at[chip], in_b.at[chip]
                ).start()

            @pl.when(chip != owner)
            def _():
                remote(
                    piece(combc, owner, rows),
                    bbuf.at[chip],
                    deal_s.at[owner],
                    in_b.at[chip],
                    seq=2 * owner + core,
                ).start()

    lax.fori_loop(0, owners, scatter, 0)

    def take(j, carry):
        arrived(bbuf.at[j], in_b.at[j])
        return carry

    lax.fori_loop(0, chips, take, 0)
    state = jnp.zeros((rows, DK), F32)
    batch = max(1, chips // 2)
    for start in range(0, chips, batch):
        for t in range(start, start + batch):
            j = chips - 1 - t
            sbuf[t] = state
            state = dot3(split(state), (ah_ref[j], al_ref[j])) + bbuf[j]
        deliver(
            chips, chip, core, rows, sbuf, gin, send_sem, in_sem,
            [(t, chips - 1 - t) for t in range(start, start + batch)],
        )

    @pl.when(me < owners)
    def _():
        gather[me] = red_ref[pl.ds(me * share, share)]

        def add(s, total):
            return total + gather[s]

        def got(s, carry):
            other = lax.rem(me + s, count)
            arrived(gather.at[other], red_r.at[other])
            return carry

        lax.fori_loop(1, count, got, 0)
        total = lax.fori_loop(0, count, add, jnp.zeros((share, RANK, 128), F32))
        zbuf[line] = total
        for peer in peers:
            remote(zbuf.at[line], zbuf.at[line], z_s.at[peer], z_r.at[line], head=peer).start()

    for n in range(OWN):
        for p in range(per):
            arrived(piece(gin, n * per + p, rows), in_sem.at[n * per + p])
        leaving = gin[n]
        between = dot3(split(leaving), split(second_ref[n])) + secondc[n]
        s_ref[mine + n] = jnp.where(lead, between, leaving)
        stage[n] = jnp.where(lead, leaving, between)
        remote(stage.at[n], s_ref.at[mine + n], fix_s.at[n], fix_r.at[n], seq=sibling).start()

    @pl.when(me < owners)
    def _():
        for peer in peers:
            arrived(zbuf.at[peer], z_r.at[peer])
        every = zbuf[0]
        for z in range(1, heads):
            every = every + zbuf[z]
        block = me * share + lax.broadcasted_iota(jnp.int32, (share, RANK, 128), 0)
        own = fin_ref.at[pl.ds(me * share, share)]
        own[...] = jnp.where(block < HEADS, zbuf[line], every)

        def tell(s, carry):
            other = lax.rem(me + s, count)
            remote(own, own, fin_s.at[other], fin_r.at[me], seq=other).start()
            return carry

        lax.fori_loop(1, count, tell, 0)

    for n in range(OWN):
        arrived(sibc.at[n], pair_s.at[n])
        arrived(stage.at[n], fix_s.at[n])
        arrived(s_ref.at[theirs + n], fix_r.at[n])

    def settle(s, carry):
        other = lax.rem(chip + s, chips)
        arrived(bbuf.at[other], deal_s.at[other])
        arrived(sbuf.at[other], send_sem.at[other])
        return carry

    lax.fori_loop(1, chips, settle, 0)

    def heard(o, carry):
        @pl.when(o != me)
        def _():
            arrived(gather.at[o], red_s.at[o])
            arrived(fin_ref.at[pl.ds(o * share, share)], fin_r.at[o])

        return carry

    lax.fori_loop(0, owners, heard, 0)

    @pl.when(me < owners)
    def _():
        for peer in peers:
            arrived(zbuf.at[peer], z_s.at[peer])

        def told(s, carry):
            other = lax.rem(me + s, count)
            arrived(fin_ref.at[pl.ds(me * share, share)], fin_s.at[other])
            return carry

        lax.fori_loop(1, count, told, 0)


VM = pl.BlockSpec(memory_space=pltpu.VMEM)
SM = pl.BlockSpec(memory_space=pltpu.SMEM)
LIMIT = 56 * 1024 * 1024


def struct(*shape, dtype=F32):
    return jax.ShapeDtypeStruct(shape, dtype)


DMA = pltpu.SemaphoreType.DMA


def forward_scan(a, bt, count):
    chips = count // 2
    rows = OWN * DV // chips
    half = pltpu.VMEM((OWN, DK, DV), F32)
    part = pltpu.VMEM((chips, rows, DK), F32)
    return pl.pallas_call(
        functools.partial(forward_kernel, count),
        out_shape=(
            struct(HEADS, DV, DK),
            struct(chips, DK, DK, dtype=BF16),
            struct(chips, DK, DK, dtype=BF16),
            struct(OWN, DK, DK),
            struct(OWN, DK, DK),
        ),
        in_specs=[VM] * 2,
        out_specs=(VM,) * 5,
        scratch_shapes=[half] * 5
        + [pltpu.VMEM((chips, DK, DK), F32), part, part, half, half]
        + [DMA((OWN,))] * 4
        + [DMA((chips,))] * 6
        + [DMA((OWN,))] * 2,
        compiler_params=pltpu.CompilerParams(
            collective_id=0, has_side_effects=True, vmem_limit_bytes=LIMIT
        ),
        name="forward_states",
    )(a, bt)


def backward_scan(ct, high, low, first, second, red, count, heads):
    chips = count // 2
    rows = OWN * DV // chips
    half = pltpu.VMEM((OWN, DK, DV), F32)
    part = pltpu.VMEM((chips, rows, DK), F32)
    blocks = red.shape[0]
    share = -(-blocks // count)
    return pl.pallas_call(
        functools.partial(backward_kernel, count, heads, blocks),
        out_shape=(struct(HEADS, DV, DK), struct(*red.shape)),
        in_specs=[VM] * 6,
        out_specs=(VM, VM),
        scratch_shapes=[half] * 3
        + [part, part, half, half]
        + [
            pltpu.VMEM((count, share, RANK, 128), F32),
            pltpu.VMEM((heads, share, RANK, 128), F32),
        ]
        + [DMA((OWN,))] * 2
        + [DMA((chips,))] * 4
        + [DMA((OWN,))] * 2
        + [DMA((count,))] * 2
        + [DMA((heads,))] * 2
        + [DMA((count,))] * 2,
        compiler_params=pltpu.CompilerParams(
            collective_id=1, has_side_effects=True, vmem_limit_bytes=LIMIT
        ),
        name="state_gradients",
    )(ct, high, low, first, second, red)


def body(
    query_matrix_rows,
    key_matrix_rows,
    value_matrix_rows,
    write_strength,
    forget_gate_code,
    value_to_key_head,
    output_norm_gain,
    output_weight,
    adapter_lowering,
    adapter_raising,
    output_gradient,
):
    count = lax.axis_size("seq")
    blocks = HEADS + output_gradient.shape[1] // 128
    params = pltpu.CompilerParams(vmem_limit_bytes=LIMIT)
    per_head = struct(HEADS, TOK, DK)
    a, bt, w, u, e, o, zt, yh, yl, gn, gr, rows, cols = pl.pallas_call(
        local_kernel,
        out_shape=(
            struct(HEADS, DK, DK),
            struct(HEADS, DV, DK),
            per_head,
            per_head,
            per_head,
            per_head,
            struct(HEADS, DK, TOK),
            struct(HEADS, TOK, TOK, dtype=BF16),
            struct(HEADS, TOK, TOK, dtype=BF16),
            struct(TOK, HEADS * DV),
            struct(RANK, TOK),
            struct(128, TOK),
            struct(TOK, 128),
        ),
        in_specs=[SM] + [VM] * 9,
        out_specs=(VM,) * 13,
        scratch_shapes=[
            pltpu.VMEM((KEYS, TOK, DK), BF16),
            pltpu.VMEM((KEYS, DK, TOK), BF16),
            pltpu.VMEM((KEYS, TOK, DK), BF16),
            pltpu.VMEM((KEYS, TOK, TOK), F32),
            pltpu.VMEM((KEYS, TOK, TOK), F32),
        ],
        compiler_params=params,
        name="local_pass",
    )(
        value_to_key_head,
        query_matrix_rows,
        key_matrix_rows,
        value_matrix_rows,
        write_strength,
        forget_gate_code,
        output_gradient,
        output_weight,
        adapter_lowering,
        adapter_raising,
    )
    s0, high, low, first, second = forward_scan(a, bt, count)
    ct, xt, uf, ft, dq, red = pl.pallas_call(
        middle_kernel,
        out_shape=(
            struct(HEADS, DV, DK),
            struct(HEADS, DV, TOK),
            per_head,
            struct(HEADS, DK, TOK),
            struct(TOK, KEYS * DK),
            struct(blocks, RANK, 128),
        ),
        in_specs=[SM] + [VM] * 16,
        out_specs=(VM,) * 6,
        scratch_shapes=[
            pltpu.VMEM((KEYS, TOK, DK), BF16),
            pltpu.VMEM((KEYS, TOK, DK), BF16),
            pltpu.VMEM((KEYS, DK, TOK), BF16),
            pltpu.VMEM((KEYS, TOK, DK), F32),
        ],
        compiler_params=params,
        name="middle_pass",
    )(
        value_to_key_head,
        s0,
        query_matrix_rows,
        key_matrix_rows,
        w,
        u,
        e,
        o,
        yh,
        yl,
        gn,
        gr,
        rows,
        cols,
        output_norm_gain.reshape(1, DV),
        output_gradient,
        adapter_lowering,
    )
    ds, fin = backward_scan(
        ct, high, low, first, second, red, count, lax.axis_size("head")
    )
    dk, dv, db, grad_down, raising_gradient = pl.pallas_call(
        last_kernel,
        out_shape=(
            struct(TOK, KEYS * DK),
            struct(TOK, HEADS * DV),
            struct(HEADS, TOK),
            struct(RANK, HEADS * DV),
            struct(RANK, output_gradient.shape[1]),
        ),
        in_specs=[SM] + [VM] * 10,
        out_specs=(VM,) * 5,
        scratch_shapes=[
            pltpu.VMEM((KEYS, TOK, DK), BF16),
            pltpu.VMEM((KEYS, DK, TOK), BF16),
            pltpu.VMEM((KEYS, TOK, DK), F32),
            pltpu.VMEM((KEYS, DK, TOK), F32),
        ],
        compiler_params=params,
        name="last_pass",
    )(value_to_key_head, ds, s0, key_matrix_rows, xt, zt, uf, ft, rows, cols, fin)
    return (dq, dk, dv, db, grad_down, raising_gradient)


def solution(mesh):
    placed = (
        P("seq", "head"),
        P("seq", "head"),
        P("seq", "head"),
        P("head", "seq"),
        P("head", "seq"),
        P("head"),
        P(),
        P("head", None),
        P(None, "head"),
        P(),
        P("seq", None),
    )
    return jax.shard_map(
        body,
        mesh=mesh,
        in_specs=placed,
        out_specs=(
            P("seq", "head"),
            P("seq", "head"),
            P("seq", "head"),
            P("head", "seq"),
            P(None, "head"),
            P(),
        ),
        check_vma=False,
    )
```

```python
import functools
import types

import jax
import jax.numpy as jnp
from jax import lax
from jax.experimental import pallas as pl
from jax.experimental.pallas import tpu as pltpu
from jax.sharding import PartitionSpec as P

DK = 128
DV = 128
TOK = 256
HALF = 128
HEADS = 8
KEYS = 4
RANK = 16
EPS = 1e-06
F32 = jnp.float32
BF16 = jnp.bfloat16
MESH = pl.DeviceIdType.MESH

NN = (((1,), (0,)), ((), ()))
NT = (((1,), (1,)), ((), ()))
TN = (((0,), (0,)), ((), ()))


def dot(x, y, form=NN):
    return lax.dot_general(x, y, form, preferred_element_type=F32)


def split(x):
    high = x.astype(BF16)
    return high, (x - high.astype(F32)).astype(BF16)


def cat(parts, axis):
    return jnp.concatenate(parts, axis=axis)


def dot3(x, y, form=NN):
    cx, cy = form[0][0][0], form[0][1][0]
    return dot(cat([x[0], x[1], x[0]], cx), cat([y[0], y[0], y[1]], cy), form)


def dot2(x, exact, form=NN):
    cx, cy = form[0][0][0], form[0][1][0]
    return dot(cat(list(x), cx), cat([exact, exact], cy), form)


def dot2r(exact, y, form=NN):
    cx, cy = form[0][0][0], form[0][1][0]
    return dot(cat([exact, exact], cx), cat(list(y), cy), form)


def square(x, y):
    right = cat([cat([y[0], y[1]], 1), cat([y[0], jnp.zeros_like(y[1])], 1)], 0)
    both = dot(cat([x[0], x[1]], 1), right)
    return both[:, :HALF] + both[:, HALF:]


def grid_of(rows, columns):
    return (
        lax.broadcasted_iota(jnp.int32, (rows, columns), 0),
        lax.broadcasted_iota(jnp.int32, (rows, columns), 1),
    )


def inverses(blocks):
    row, col = grid_of(HALF, HALF)
    eye = jnp.where(row == col, 1.0, 0.0).astype(F32)
    pairs = ((row >> 1) == (col >> 1)) & (row > col)
    found = [eye - jnp.where(pairs, block, 0.0) for block in blocks]
    for level in range(1, 7):
        here = ((row >> (level + 1)) == (col >> (level + 1))) & ((row >> level) > (col >> level))
        halves = [split(x) for x in found]
        inner = [
            split(square(split(jnp.where(here, block, 0.0)), x))
            for block, x in zip(blocks, halves)
        ]
        found = [x - square(h, y) for x, h, y in zip(found, halves, inner)]
    return found


ROW_R, ROW_C, ROW_P, ROW_G, ROW_BG, ROW_AG, ROW_KEY = 0, 8, 16, 24, 32, 40, 48


def last_kernel(
    which,
    ds_ref,
    s0_ref,
    k_ref,
    xt_ref,
    zt_ref,
    u_ref,
    ft_ref,
    rows_ref,
    cols_ref,
    fin_ref,
    dqin_ref,
    dq_ref,
    dk_ref,
    dv_ref,
    db_ref,
    down_ref,
    raise_ref,
    k4,
    kt4,
    acc4,
    acct4,
):
    for m in range(KEYS):
        at = slice(m * DK, (m + 1) * DK)
        k4[m] = k_ref[:, at]
        kt4[m] = k_ref[:, at].T
    acc4[...] = jnp.zeros_like(acc4)
    acct4[...] = jnp.zeros_like(acct4)
    dq_ref[...] = dqin_ref[...]
    for n in range(HEADS):
        down_ref[:, n * 128 : (n + 1) * 128] = fin_ref[n]
    for n in range(raise_ref.shape[1] // 128):
        raise_ref[:, n * 128 : (n + 1) * 128] = fin_ref[HEADS + n]
    row, col = grid_of(TOK, TOK)
    for h in range(HEADS):
        m = which[h] % KEYS
        dst = ds_ref[h]
        drt = xt_ref[h] + dot3(split(dst), split(zt_ref[h]))
        dr = drt.T
        dv_ref[:, h * DV : (h + 1) * DV] = dr
        drs, us = split(dr), split(u_ref[h])
        dl = split(jnp.where(row > col, -dot3(drs, us, NT), 0.0))
        kt = kt4[m].astype(F32)
        rk = split(kt * rows_ref[ROW_R + h : ROW_R + h + 1, :])
        ck = split(k4[m].astype(F32) * cols_ref[:, ROW_C + h : ROW_C + h + 1])
        last = rows_ref[ROW_G + h : ROW_G + h + 1, TOK - 1 : TOK]
        f = ft_ref[h] + dot3(rk, dl) + last * dot3(split(dst.T), us, NT)
        db_ref[h : h + 1, :] = (
            jnp.sum(kt * f, axis=0, keepdims=True) * rows_ref[ROW_AG + h : ROW_AG + h + 1, :]
        )
        own = dot3(dl, ck) - dot3(drs, split(s0_ref[h]))
        acc4[m] = acc4[m] + own * cols_ref[:, ROW_G + h : ROW_G + h + 1]
        acct4[m] = acct4[m] + f * rows_ref[ROW_BG + h : ROW_BG + h + 1, :]
    for m in range(KEYS):
        total = acc4[m] + acct4[m].T
        k = k4[m].astype(F32)
        inv = cols_ref[:, ROW_KEY + m : ROW_KEY + m + 1]
        along = jnp.sum(total * k, axis=-1, keepdims=True)
        dk_ref[:, m * DK : (m + 1) * DK] = inv * (total - k * (inv * inv * along))


def remote(src, dst, ssem, rsem, **where):
    return pltpu.make_async_remote_copy(
        src_ref=src,
        dst_ref=dst,
        send_sem=ssem,
        recv_sem=rsem,
        device_id=where,
        device_id_type=MESH,
    )


def arrived(ref, sem):
    pltpu.make_async_copy(ref, ref, sem).wait()


OWN = HEADS // 2


def place(count):
    me = lax.axis_index("seq")
    core = lax.rem(me, 2)
    return me, me // 2, core, me + 1 - 2 * core


def piece(ref, owner, rows):
    per = DV // rows
    return ref.at[owner // per, pl.ds(pl.multiple_of(lax.rem(owner, per) * rows, rows), rows)]


def turns(chip, chips, act):
    def one(s, carry):
        act(lax.rem(chip + s, chips))
        return carry

    lax.fori_loop(0, chips, one, 0)


def deliver(chips, chip, core, rows, sbuf, into, send_sem, in_sem):
    mine = chip - core * (chips // 2)

    def act(j):
        @pl.when(chip == j)
        def _():
            pltpu.make_async_copy(sbuf.at[j], piece(into, mine, rows), in_sem.at[mine]).start()

        @pl.when(chip != j)
        def _():
            remote(
                sbuf.at[j],
                piece(into, mine, rows),
                send_sem.at[j],
                in_sem.at[mine],
                seq=2 * j + core,
            ).start()

    turns(chip, chips, act)


def table(r):
    lane = lax.broadcasted_iota(jnp.int32, (HEADS, TOK), 1)
    gamma = 1.0 - r.code[...].astype(F32) * 2.0 ** (-20)
    step = 1
    while step < TOK:
        gamma = gamma * jnp.where(lane >= step, pltpu.roll(gamma, step, 1), 1.0)
        step *= 2
    back = 1.0 / gamma
    ones = jnp.ones((8, DK), BF16)
    r.rows[...] = jnp.zeros_like(r.rows)
    for m in range(KEYS):
        at = slice(m * DK, (m + 1) * DK)
        k = r.k[:, at]
        q = r.q[:, at]
        r.k4[m] = k
        r.q4[m] = q
        r.kt4[m] = k.T
        r.qt4[m] = q.T
        r.kk4[m] = dot(k, k, NT)
        r.qk4[m] = dot(q, k, NT)
        kf, qf = k.astype(F32), q.astype(F32)
        ksum = dot2r(ones, split(kf * kf), NT)[0:1]
        qsum = dot2r(ones, split(qf * qf), NT)[0:1]
        r.rows[ROW_KEY + m : ROW_KEY + m + 1, :] = lax.rsqrt(ksum + EPS)
        r.rows[ROW_KEY + KEYS + m : ROW_KEY + KEYS + m + 1, :] = lax.rsqrt(qsum + EPS)
    rate = r.rate[...]
    for h in range(HEADS):
        m = r.which[h] % KEYS
        a = r.rows[pl.ds(ROW_KEY + m, 1), :]
        b = r.rows[pl.ds(ROW_KEY + KEYS + m, 1), :] * DK ** (-0.5)
        g, i, w = gamma[h : h + 1], back[h : h + 1], rate[h : h + 1]
        for at, value in (
            (ROW_R, g * a),
            (ROW_C, a * w * i),
            (ROW_P, g * b),
            (ROW_G, g),
            (ROW_BG, w * i),
            (ROW_AG, a * i),
        ):
            r.rows[at + h : at + h + 1, :] = value
    r.cols[...] = r.rows[...].T


def column(r, at):
    return r.cols[:, at : at + 1]


def line_of(r, at):
    return r.rows[at : at + 1, :]


def summaries(r, heads):
    row, col = grid_of(TOK, TOK)
    srow, scol = grid_of(HALF, HALF)
    eye = jnp.where(srow == scol, 1.0, 0.0).astype(F32)
    blocks, corners = [], []
    for h in heads:
        m = r.which[h] % KEYS
        strict = jnp.where(
            row > col, r.kk4[m] * column(r, ROW_R + h) * line_of(r, ROW_C + h), 0.0
        )
        blocks += [strict[:HALF, :HALF], strict[HALF:, HALF:]]
        corners.append(split(strict[HALF:, :HALF]))
    found = inverses(blocks)
    for n, h in enumerate(heads):
        m = r.which[h] % KEYS
        first, second = split(found[2 * n]), split(found[2 * n + 1])
        corner = split(-square(second, split(square(corners[n], first))))
        blank = jnp.zeros((HALF, HALF), BF16)
        t = tuple(
            cat([cat([first[i], blank], 1), cat([corner[i], second[i]], 1)], 0) for i in range(2)
        )
        r.th[h] = t[0]
        r.tl[h] = t[1]
        final = r.rows[ROW_G + h : ROW_G + h + 1, TOK - 1 : TOK]
        ended = split(r.kt4[m].astype(F32) * (line_of(r, ROW_C + h) * final))
        zt = dot3(ended, t)
        zs = split(zt)
        r.zt[h] = zt
        g = split(r.k4[m].astype(F32) * column(r, ROW_R + h))
        r.a[h] = final * eye - dot3(zs, g)
        r.b[h] = dot2r(r.v[:, h * DV : (h + 1) * DV].T, zs, NT)


def readings(r):
    row, col = grid_of(TOK, TOK)
    for h in range(HEADS):
        m = r.which[h] % KEYS
        t = (r.th[h], r.tl[h])
        q = r.q4[m].astype(F32)
        g = split(r.k4[m].astype(F32) * column(r, ROW_R + h))
        pair = cat([g[0], r.v[:, h * DV : (h + 1) * DV]], 1)
        wu = dot2(t, pair)
        r.w[h] = wu[:, :DK] + dot(t[0], g[1])
        r.u[h] = wu[:, DK:]
        mixing = jnp.where(
            row >= col, r.qk4[m] * column(r, ROW_P + h) * line_of(r, ROW_C + h), 0.0
        )
        y = split(dot3(split(mixing), t))
        r.yh[h] = y[0]
        r.yl[h] = y[1]
        eo = dot2(y, pair)
        r.e[h] = q * column(r, ROW_P + h) - (eo[:, :DK] + dot(y[0], g[1]))
        r.o[h] = eo[:, DK:]


def projections(r):
    rs = split(r.lift[...])
    both = dot(cat(list(rs), 0), r.og[...], NT)
    grt = both[:RANK] + both[RANK:]
    gs = split(2.0 * grt)
    r.grh[...] = gs[0]
    r.grl[...] = gs[1]
    for h in range(HEADS):
        at = slice(h * DV, (h + 1) * DV)
        low = dot3(gs, split(r.lower[:, at]), TN)
        r.gn[:, at] = dot(r.og[...], r.weight[at, :], NT) + low


def outputs(r, heads):
    gain = r.gain[...]
    for h in heads:
        es = split(r.e[h])
        o = r.o[h] + dot3(es, split(r.s0[h]), NT)
        scale = lax.rsqrt(jnp.mean(o * o, axis=-1, keepdims=True) + EPS)
        gn = r.gn[:, h * DV : (h + 1) * DV] * gain
        tail = jnp.mean(gn * o, axis=-1, keepdims=True)
        do = scale * gn - o * (scale * scale * scale * tail)
        normed = split(o * scale * gain)
        r.nh[h] = normed[0]
        r.nl[h] = normed[1]
        r.do[h] = do
        dts = split(do.T)
        r.dth[h] = dts[0]
        r.dtl[h] = dts[1]
        r.ct[h] = dot3(dts, es)


def adapters(r):
    gs = (r.grh[...], r.grl[...])
    rank = jnp.zeros((RANK, TOK), F32)
    for h in range(HEADS):
        normed = (r.nh[h], r.nl[h])
        rank = rank + dot3(split(r.lower[:, h * DV : (h + 1) * DV]), normed, NT)
        r.red[h] = dot3(gs, normed)
    lift = 2.0 * dot2(split(rank), r.og[...])
    for n in range(lift.shape[1] // 128):
        r.red[HEADS + n] = lift[:, n * 128 : (n + 1) * 128]


def mixtures(r):
    row, col = grid_of(TOK, TOK)
    for h in range(HEADS):
        m = r.which[h] % KEYS
        ss = split(r.s0[h])
        u = r.u[h] - dot3(split(r.w[h]), ss, NT)
        r.uf[h] = u
        r.xt[h] = dot3((r.dth[h], r.dtl[h]), (r.yh[h], r.yl[h]))
        ds, us = split(r.do[h]), split(u)
        dp = split(jnp.where(row >= col, dot3(ds, us, NT), 0.0))
        ck = split(r.k4[m].astype(F32) * column(r, ROW_C + h))
        r.dqh[h] = (dot3(ds, ss) + dot3(dp, ck)) * column(r, ROW_G + h)
        pq = split(r.qt4[m].astype(F32) * line_of(r, ROW_P + h))
        r.ft[h] = dot3(pq, dp)
    for m in range(KEYS):
        one, two = 0, 0
        for h in range(HEADS):
            two = jnp.where(r.which[h] % KEYS == m, h, two)
            one = jnp.where(r.which[HEADS - 1 - h] % KEYS == m, HEADS - 1 - h, one)
        total = r.dqh[one] + r.dqh[two]
        q = r.q4[m].astype(F32)
        inv = column(r, ROW_KEY + KEYS + m)
        along = jnp.sum(total * q, axis=-1, keepdims=True)
        r.dq[:, m * DK : (m + 1) * DK] = (DK ** (-0.5) * inv) * (total - q * (inv * inv * along))


def main_kernel(count, lines, blocks, names, *refs):
    r = types.SimpleNamespace(**dict(zip(names, refs)))
    chips = count // 2
    owners = chips // 2
    rows = OWN * DV // owners
    per = DV // rows
    me, chip, core, sibling = place(count)
    mine, theirs = core * OWN, (1 - core) * OWN
    lead = core == 0
    holding = chip // owners == core
    line = lax.axis_index("head")
    share = -(-blocks // chips)
    holders = blocks // share
    summing = jnp.logical_and(chip // owners != core, chip < holders)
    peers = [lax.rem(line + s, lines) for s in range(1, lines)]
    barrier = pltpu.get_barrier_semaphore()

    def hello(s, carry):
        other = lax.rem(me + s, count)
        pl.semaphore_signal(barrier, inc=1, device_id={"seq": other}, device_id_type=MESH)
        return carry

    lax.fori_loop(1, count, hello, 0)
    for peer in peers:
        pl.semaphore_signal(barrier, inc=1, device_id={"head": peer}, device_id_type=MESH)

    table(r)
    for half in range(2):
        summaries(r, range(half * OWN, (half + 1) * OWN))
        if half == 0:
            pl.semaphore_wait(barrier, count - 1 + len(peers))

        @pl.when(core != half)
        def _():
            for n in range(OWN):
                h = half * OWN + n
                remote(
                    r.a.at[h], r.siba.at[n], r.pair_as.at[n], r.pair_a.at[n], seq=sibling
                ).start()
                remote(
                    r.b.at[h], r.sibb.at[n], r.pair_bs.at[n], r.pair_b.at[n], seq=sibling
                ).start()

    for n in range(OWN):
        arrived(r.siba.at[n], r.pair_a.at[n])
        arrived(r.sibb.at[n], r.pair_b.at[n])
    for n in range(OWN):
        oa, ob, ta, tb = r.a[mine + n], r.b[mine + n], r.siba[n], r.sibb[n]
        first, second = jnp.where(lead, oa, ta), jnp.where(lead, ta, oa)
        fb, sb = jnp.where(lead, ob, tb), jnp.where(lead, tb, ob)
        r.first[n] = first
        r.second[n] = second
        r.firstb[n] = fb
        ss = split(second)
        r.comb[n] = dot3(ss, split(first))
        r.combb[n] = dot3(split(fb), ss, NT) + sb

    def deal(w):
        there = core * owners + w

        @pl.when(chip == there)
        def _():
            pltpu.make_async_copy(r.comb.at[w // per], r.abuf.at[chip], r.in_a.at[chip]).start()
            pltpu.make_async_copy(
                piece(r.combb, w, rows), r.bbuf.at[chip], r.in_b.at[chip]
            ).start()

        @pl.when(chip != there)
        def _():
            device = 2 * there + core
            remote(
                r.comb.at[w // per], r.abuf.at[chip], r.deal_a.at[w], r.in_a.at[chip], seq=device
            ).start()
            remote(
                piece(r.combb, w, rows),
                r.bbuf.at[chip],
                r.deal_b.at[w],
                r.in_b.at[chip],
                seq=device,
            ).start()

    turns(lax.rem(chip, owners), owners, deal)
    readings(r)
    projections(r)

    @pl.when(holding)
    def _():
        def take(j, carry):
            arrived(r.abuf.at[j], r.in_a.at[j])
            high, low = split(r.abuf[j])
            r.ah[j] = high
            r.al[j] = low
            arrived(r.bbuf.at[j], r.in_b.at[j])
            return carry

        lax.fori_loop(0, chips, take, 0)
        state = jnp.zeros((rows, DK), F32)
        for j in range(chips):
            r.sbuf[j] = state
            state = dot3(split(state), (r.ah[j], r.al[j]), NT) + r.bbuf[j]
        deliver(chips, chip, core, rows, r.sbuf, r.gin, r.send, r.in_s)

    for w in range(owners):
        arrived(piece(r.gin, w, rows), r.in_s.at[w])
    for n in range(OWN):
        entering = r.gin[n]
        between = dot3(split(entering), split(r.first[n]), NT) + r.firstb[n]
        r.s0[mine + n] = jnp.where(lead, entering, between)
        r.stage[n] = jnp.where(lead, between, entering)
    for n in range(OWN):
        remote(
            r.stage.at[n], r.s0.at[mine + n], r.fix_s.at[n], r.fix_r.at[n], seq=sibling
        ).start()
    for n in range(OWN):
        arrived(r.s0.at[theirs + n], r.fix_r.at[n])

    for half in range(2):
        outputs(r, range(half * OWN, (half + 1) * OWN))

        @pl.when(core != half)
        def _():
            for n in range(OWN):
                remote(
                    r.ct.at[half * OWN + n],
                    r.sibc.at[n],
                    r.pair_cs.at[n],
                    r.pair_c.at[n],
                    seq=sibling,
                ).start()

    for n in range(OWN):
        arrived(r.sibc.at[n], r.pair_c.at[n])
    for n in range(OWN):
        oc, tc = r.ct[mine + n], r.sibc[n]
        first, second = jnp.where(lead, oc, tc), jnp.where(lead, tc, oc)
        r.secondc[n] = second
        r.combc[n] = dot3(split(second), split(r.first[n])) + first

    def deal_back(w):
        there = core * owners + w

        @pl.when(chip == there)
        def _():
            pltpu.make_async_copy(
                piece(r.combc, w, rows), r.cbuf.at[chip], r.in_c.at[chip]
            ).start()

        @pl.when(chip != there)
        def _():
            remote(
                piece(r.combc, w, rows),
                r.cbuf.at[chip],
                r.deal_c.at[w],
                r.in_c.at[chip],
                seq=2 * there + core,
            ).start()

    turns(lax.rem(chip, owners), owners, deal_back)
    adapters(r)

    def holder(q):
        return 2 * q + 1 - q // owners

    def scatter(q):
        @pl.when(jnp.logical_and(q < holders, holder(q) != me))
        def _():
            remote(
                r.red.at[pl.ds(q * share, share)],
                r.gather.at[me],
                r.red_s.at[q],
                r.red_r.at[me],
                seq=holder(q),
            ).start()

    turns(chip, chips, scatter)
    mixtures(r)

    @pl.when(holding)
    def _():
        def take(j, carry):
            arrived(r.cbuf.at[j], r.in_c.at[j])
            return carry

        lax.fori_loop(0, chips, take, 0)
        state = jnp.zeros((rows, DK), F32)
        for t in range(chips):
            j = chips - 1 - t
            r.tbuf[j] = state
            state = dot3(split(state), (r.ah[j], r.al[j])) + r.cbuf[j]
        deliver(chips, chip, core, rows, r.tbuf, r.gout, r.send_g, r.in_g)

    @pl.when(summing)
    def _():
        r.gather[me] = r.red[pl.ds(chip * share, share)]

        def got(s, carry):
            other = lax.rem(me + s, count)
            arrived(r.gather.at[other], r.red_r.at[other])
            return carry

        def add(s, total):
            return total + r.gather[s]

        lax.fori_loop(1, count, got, 0)
        r.zbuf[line] = lax.fori_loop(0, count, add, jnp.zeros((share, RANK, 128), F32))
        for peer in peers:
            remote(
                r.zbuf.at[line], r.zbuf.at[line], r.z_s.at[peer], r.z_r.at[line], head=peer
            ).start()
        for peer in peers:
            arrived(r.zbuf.at[peer], r.z_r.at[peer])
        every = r.zbuf[0]
        for z in range(1, lines):
            every = every + r.zbuf[z]
        block = chip * share + lax.broadcasted_iota(jnp.int32, (share, RANK, 128), 0)
        own = r.fin.at[pl.ds(chip * share, share)]
        own[...] = jnp.where(block < HEADS, r.zbuf[line], every)

        def tell(s, carry):
            other = lax.rem(me + s, count)
            remote(own, own, r.fin_s.at[other], r.fin_r.at[chip], seq=other).start()
            return carry

        lax.fori_loop(1, count, tell, 0)

    for w in range(owners):
        arrived(piece(r.gout, w, rows), r.in_g.at[w])
    for n in range(OWN):
        leaving = r.gout[n]
        between = dot3(split(leaving), split(r.second[n])) + r.secondc[n]
        r.ds[mine + n] = jnp.where(lead, between, leaving)
        r.stageg[n] = jnp.where(lead, leaving, between)
    for n in range(OWN):
        remote(
            r.stageg.at[n], r.ds.at[mine + n], r.fix_gs.at[n], r.fix_g.at[n], seq=sibling
        ).start()

    for n in range(OWN):
        arrived(r.siba.at[n], r.pair_as.at[n])
        arrived(r.sibb.at[n], r.pair_bs.at[n])
        arrived(r.sibc.at[n], r.pair_cs.at[n])
        arrived(r.stage.at[n], r.fix_s.at[n])

    def dealt(w):
        @pl.when(chip != core * owners + w)
        def _():
            arrived(r.abuf.at[w], r.deal_a.at[w])
            arrived(r.bbuf.at[w], r.deal_b.at[w])
            arrived(r.cbuf.at[w], r.deal_c.at[w])

    turns(lax.rem(chip, owners), owners, dealt)

    @pl.when(holding)
    def _():
        def settle(s, carry):
            other = lax.rem(chip + s, chips)
            arrived(r.sbuf.at[other], r.send.at[other])
            arrived(r.tbuf.at[other], r.send_g.at[other])
            return carry

        lax.fori_loop(1, chips, settle, 0)

    def heard(q):
        @pl.when(jnp.logical_and(q < holders, holder(q) != me))
        def _():
            arrived(r.gather.at[q], r.red_s.at[q])
            arrived(r.fin.at[pl.ds(q * share, share)], r.fin_r.at[q])

    turns(chip, chips, heard)

    @pl.when(summing)
    def _():
        for peer in peers:
            arrived(r.zbuf.at[peer], r.z_s.at[peer])

        def told(s, carry):
            other = lax.rem(me + s, count)
            arrived(r.fin.at[pl.ds(chip * share, share)], r.fin_s.at[other])
            return carry

        lax.fori_loop(1, count, told, 0)

    for n in range(OWN):
        arrived(r.stageg.at[n], r.fix_gs.at[n])
        arrived(r.ds.at[theirs + n], r.fix_g.at[n])


VM = pl.BlockSpec(memory_space=pltpu.VMEM)
SM = pl.BlockSpec(memory_space=pltpu.SMEM)
LIMIT = 56 * 1024 * 1024


def struct(*shape, dtype=F32):
    return jax.ShapeDtypeStruct(shape, dtype)


DMA = pltpu.SemaphoreType.DMA


def body(
    query_matrix_rows,
    key_matrix_rows,
    value_matrix_rows,
    write_strength,
    forget_gate_code,
    value_to_key_head,
    output_norm_gain,
    output_weight,
    adapter_lowering,
    adapter_raising,
    output_gradient,
):
    count, lines = lax.axis_size("seq"), lax.axis_size("head")
    width = output_gradient.shape[1]
    blocks = HEADS + width // 128
    chips = count // 2
    rows = OWN * DV // (chips // 2)
    share = -(-blocks // chips)
    arguments = dict(
        which=value_to_key_head,
        q=query_matrix_rows,
        k=key_matrix_rows,
        v=value_matrix_rows,
        rate=write_strength,
        code=forget_gate_code,
        gain=output_norm_gain.reshape(1, DV),
        weight=output_weight,
        lower=adapter_lowering,
        lift=adapter_raising,
        og=output_gradient,
    )
    results = dict(
        s0=(HEADS, DV, DK),
        ds=(HEADS, DV, DK),
        xt=(HEADS, DV, TOK),
        zt=(HEADS, DK, TOK),
        uf=(HEADS, TOK, DV),
        ft=(HEADS, DK, TOK),
        rows=(128, TOK),
        cols=(TOK, 128),
        fin=(blocks, RANK, 128),
        dq=(TOK, KEYS * DK),
    )

    def full(*shape):
        return pltpu.VMEM(shape, F32)

    def small(*shape):
        return pltpu.VMEM(shape, BF16)

    scratch = dict(
        k4=small(KEYS, TOK, DK),
        q4=small(KEYS, TOK, DK),
        kt4=small(KEYS, DK, TOK),
        qt4=small(KEYS, DK, TOK),
        kk4=full(KEYS, TOK, TOK),
        qk4=full(KEYS, TOK, TOK),
        gn=full(TOK, HEADS * DV),
        red=full(blocks, RANK, 128),
        grh=small(RANK, TOK),
        grl=small(RANK, TOK),
        ah=small(chips, DK, DK),
        al=small(chips, DK, DK),
        abuf=full(chips, DK, DK),
        gather=full(count, share, RANK, 128),
        zbuf=full(lines, share, RANK, 128),
    )
    scratch |= {name: small(HEADS, TOK, TOK) for name in ("th", "tl", "yh", "yl")}
    scratch |= {name: full(HEADS, TOK, DK) for name in ("w", "u", "e", "o", "do", "dqh")}
    scratch |= {name: small(HEADS, TOK, DV) for name in ("nh", "nl")}
    scratch |= {name: small(HEADS, DV, TOK) for name in ("dth", "dtl")}
    scratch |= {name: full(HEADS, DK, DV) for name in ("a", "b", "ct")}
    scratch |= {
        name: full(OWN, DK, DV)
        for name in (
            ("siba", "sibb", "sibc", "comb", "combb", "combc", "first", "second")
            + ("firstb", "secondc", "gin", "gout", "stage", "stageg")
        )
    }
    scratch |= {name: full(chips, rows, DK) for name in ("bbuf", "cbuf", "sbuf", "tbuf")}
    for number, those in (
        (OWN, ("pair_a", "pair_b", "pair_c", "pair_as", "pair_bs", "pair_cs")),
        (OWN, ("fix_s", "fix_r", "fix_gs", "fix_g")),
        (chips, ("deal_a", "deal_b", "deal_c", "in_a", "in_b", "in_c")),
        (chips, ("send", "send_g", "in_s", "in_g", "red_s", "fin_r")),
        (count, ("red_r", "fin_s")),
        (lines, ("z_s", "z_r")),
    ):
        scratch |= {name: pltpu.SemaphoreType.DMA((number,)) for name in those}
    names = (*arguments, *results, *scratch)
    found = pl.pallas_call(
        functools.partial(main_kernel, count, lines, blocks, names),
        out_shape=tuple(struct(*shape) for shape in results.values()),
        in_specs=[SM] + [VM] * (len(arguments) - 1),
        out_specs=(VM,) * len(results),
        scratch_shapes=list(scratch.values()),
        compiler_params=pltpu.CompilerParams(
            collective_id=0, has_side_effects=True, vmem_limit_bytes=LIMIT
        ),
        name="main_pass",
    )(*arguments.values())
    got = dict(zip(results, found))
    dq, dk, dv, db, grad_down, raising_gradient = pl.pallas_call(
        last_kernel,
        out_shape=(
            struct(TOK, KEYS * DK),
            struct(TOK, KEYS * DK),
            struct(TOK, HEADS * DV),
            struct(HEADS, TOK),
            struct(RANK, HEADS * DV),
            struct(RANK, width),
        ),
        in_specs=[SM] + [VM] * 11,
        out_specs=(VM,) * 6,
        scratch_shapes=[
            pltpu.VMEM((KEYS, TOK, DK), BF16),
            pltpu.VMEM((KEYS, DK, TOK), BF16),
            pltpu.VMEM((KEYS, TOK, DK), F32),
            pltpu.VMEM((KEYS, DK, TOK), F32),
        ],
        compiler_params=pltpu.CompilerParams(vmem_limit_bytes=LIMIT),
        name="last_pass",
    )(
        value_to_key_head,
        got["ds"],
        got["s0"],
        key_matrix_rows,
        *(got[name] for name in ("xt", "zt", "uf", "ft", "rows", "cols", "fin", "dq")),
    )
    return (dq, dk, dv, db, grad_down, raising_gradient)


def solution(mesh):
    placed = (
        P("seq", "head"),
        P("seq", "head"),
        P("seq", "head"),
        P("head", "seq"),
        P("head", "seq"),
        P("head"),
        P(),
        P("head", None),
        P(None, "head"),
        P(),
        P("seq", None),
    )
    return jax.shard_map(
        body,
        mesh=mesh,
        in_specs=placed,
        out_specs=(
            P("seq", "head"),
            P("seq", "head"),
            P("seq", "head"),
            P("head", "seq"),
            P(None, "head"),
            P(),
        ),
        check_vma=False,
    )
```
